32 devices in a mesh: rows: 8 (over z, x), cols: 4 (over y, core).
Axes of the slice: x: 2, y: 2, z: 4, core: 2. Of those that a mesh axis runs over, the one named last changes fastest.
Arguments:
- h_blocks: float32 [64, 48, 64, 64], P('rows', 'cols'), may hold values from -0.109375 to 0.109375
- p_blocks: float32 [64, 48, 64, 64], P('rows', 'cols'), may hold values from -0.109375 to 0.109375
- h_fetch: int32 [8, 8, 2], P('rows'), may hold values from 0 to 7
- p_fetch: int32 [8, 8, 2], P('rows'), may hold values from 0 to 7
- h_slot: int32 [64, 48], P('rows'), may hold values from 0 to 15
- p_slot: int32 [64, 48], P('rows'), may hold values from 0 to 15
- p_panel: float32 [4096, 1024], P('rows', 'cols'), may hold values from -6 to 6
Outputs:
- w_panel: float32 [4096, 1024], P('rows', 'cols')
The draws below stay inside these ranges and needn't reach their ends.
Inputs may be any that keep to these rules, and one draw needn't show every extreme that they name: `p_fetch`: local block rows of the owner. `h_slot`: slot 2 * o + c names entry c of the owner o's fetch list. `p_slot`: slot 2 * o + c names entry c of the owner o's fetch list.
All inputs are finite; a program needn't handle non-finite values.
Results may differ from the reference program's by a relative error of at most 0.000098.
Values sent between devices are 32-bit elements; how exact they have to be, the bound alone decides.
A program may use at most 128 MiB of HBM per device.

```python
import jax
import jax.numpy as jnp
from jax import lax

B = 64
NB_DEV = 8
KB = 48
CAP = 2
NBR = 64
SLOTS = 16
PC = 16
N_ROWS = 8


def set_ends(array, own_key, low, top_value):
    place = [jax.random.randint(jax.random.fold_in(own_key, axis), (), 0, length) for axis, length in enumerate(array.shape)]
    widest = array.shape.index(max(array.shape))
    neighbour = place[:widest] + [(place[widest] + 1) % array.shape[widest]] + place[widest + 1:]
    return array.at[tuple(place)].set(low).at[tuple(neighbour)].set(top_value)


def shard_levels(own_key, extent, pieces, low, largest):
    loudness, own = 1.0, jax.random.fold_in(own_key, 6)
    for dim, parts in pieces:
        heights = jnp.exp(jax.random.uniform(jax.random.fold_in(own, dim), (parts,), jnp.float32, low / len(pieces), largest / len(pieces)))
        loudness = loudness * jnp.repeat(heights, extent[dim] // parts).reshape([-1 if axis == dim else 1 for axis in range(len(extent))])
    return loudness


def noise(key, shape, scale, bound, pieces=(), kind=jnp.bfloat16):
    array = scale * jax.random.normal(key, shape, jnp.float32)
    if pieces:
        array = array * shard_levels(key, shape, pieces, -0.22, 0.18)
    return jnp.clip(array, -bound, bound).astype(kind)


def setup_inputs(seed: int = 0) -> dict:
    key_of = jax.random.split(jax.random.key(seed), 8)
    return {
        "h_blocks": noise(key_of[0], (NBR, KB, B, B), (KB * B) ** -0.5, 0.109375, ((0, 8), (1, 4)), jnp.float32),
        "p_blocks": noise(key_of[1], (NBR, KB, B, B), (KB * B) ** -0.5, 0.109375, ((0, 8), (1, 4)), jnp.float32),
        "h_fetch": set_ends(jax.random.randint(key_of[2], (N_ROWS, N_ROWS, CAP), 0, NB_DEV), jax.random.fold_in(key_of[2], 1), 0, NB_DEV - 1).astype(jnp.int32),
        "p_fetch": set_ends(jax.random.randint(key_of[3], (N_ROWS, N_ROWS, CAP), 0, NB_DEV), jax.random.fold_in(key_of[3], 1), 0, NB_DEV - 1).astype(jnp.int32),
        "h_slot": set_ends(jax.random.randint(key_of[4], (NBR, KB), 0, SLOTS), jax.random.fold_in(key_of[4], 1), 0, SLOTS - 1).astype(jnp.int32),
        "p_slot": set_ends(jax.random.randint(key_of[5], (NBR, KB), 0, SLOTS), jax.random.fold_in(key_of[5], 1), 0, SLOTS - 1).astype(jnp.int32),
        "p_panel": noise(key_of[6], (NBR * B, PC * B), 1.0, 6.0, ((0, 8), (1, 4)), jnp.float32),
    }


highest = lax.Precision.HIGHEST


def sparse_product(block_list, fetch_lists, slot_lists, right_side):
    nbr_all = block_list.shape[0]
    block_size = block_list.shape[2]
    columns = right_side.shape[1]
    n_owners = fetch_lists.shape[0]
    own_rows = nbr_all // n_owners
    cap_size = fetch_lists.shape[2]
    stacked = right_side.reshape(nbr_all, block_size, columns)
    device_ids = (jnp.arange(nbr_all, dtype=jnp.int32) // own_rows).astype(jnp.int32)
    owners = (slot_lists // cap_size).astype(jnp.int32)
    position = (slot_lists % cap_size).astype(jnp.int32)
    local_row = fetch_lists[device_ids[:, None], owners, position]
    targets = (owners * own_rows + local_row).astype(jnp.int32)

    def per_row(pair_in):
        row_blocks_in, row_targets = pair_in
        return jnp.einsum("jab,jbc->ac", row_blocks_in, stacked[row_targets], precision=highest)

    result = lax.map(per_row, (block_list, targets))
    return result.reshape(nbr_all * block_size, columns)


def reference(h_blocks, p_blocks, h_fetch, p_fetch, h_slot, p_slot, p_panel):
    middle = sparse_product(h_blocks, h_fetch, h_slot, p_panel)
    return sparse_product(p_blocks, p_fetch, p_slot, middle)
```

```python
import functools

import jax
import jax.numpy as jnp
from jax import lax
from jax.experimental import pallas as pl
from jax.experimental.pallas import tpu as pltpu
from jax.sharding import PartitionSpec as P

highest = lax.Precision.HIGHEST
MESH = pl.DeviceIdType.MESH
LANES = 128


def take_kernel(indices, slab, out):
    out[...] = slab[...]


def take_slabs(slabs, indices):
    _, b, columns = slabs.shape
    slab = (1, b, columns)
    taken = pl.pallas_call(
        take_kernel,
        out_shape=jax.ShapeDtypeStruct((indices.size, b, columns), slabs.dtype),
        grid_spec=pltpu.PrefetchScalarGridSpec(
            num_scalar_prefetch=1,
            grid=(indices.size,),
            in_specs=[pl.BlockSpec(slab, lambda i, wanted: (wanted[i], 0, 0))],
            out_specs=pl.BlockSpec(slab, lambda i, wanted: (i, 0, 0)),
        ),
        name="take_slabs",
    )(indices.reshape(-1), slabs)
    return taken.reshape(*indices.shape, b, columns)


def multiply(block_list, fetch_lists, slot_lists, panel_part):
    own_rows = block_list.shape[0]
    block_size = block_list.shape[2]
    columns = panel_part.shape[1]
    wanted = lax.all_to_all(fetch_lists[0], "rows", split_axis=0, concat_axis=0, tiled=True)
    stacked = panel_part.reshape(own_rows, block_size, columns)
    packed = take_slabs(stacked, wanted)
    arrived = lax.all_to_all(packed, "rows", split_axis=0, concat_axis=0, tiled=True)
    flattened = arrived.reshape(-1, block_size, columns)
    chosen = take_slabs(flattened, slot_lists)
    result = jnp.einsum("ijab,ijbc->iac", block_list, chosen, precision=highest)
    return result.reshape(own_rows * block_size, columns)


def list_body(h_blocks, p_blocks, h_fetch, p_fetch, h_slot, p_slot, p_panel):
    gathered = (
        lax.all_gather(h_blocks, "cols", axis=1, tiled=True),
        lax.all_gather(p_blocks, "cols", axis=1, tiled=True),
    )
    middle = multiply(gathered[0], h_fetch, h_slot, p_panel)
    return multiply(gathered[1], p_fetch, p_slot, middle)


def merge_kernel(cap, h_slot, p_slot, h_blocks, p_blocks, h_out, p_out):
    i = pl.program_id(0)
    n_local, b = h_blocks.shape[1], h_blocks.shape[2]
    first = lax.axis_index("cols") * n_local
    lane_part = lax.broadcasted_iota(jnp.int32, (b, cap * b), 1) // b
    for slots, blocks, out in ((h_slot, h_blocks, h_out), (p_slot, p_blocks, p_out)):
        out[...] = jnp.zeros_like(out)
        for j in range(n_local):
            slot = slots[i, first + j]
            owner, part = slot // cap, slot % cap
            block = blocks[0, j]
            wide = jnp.concatenate([block] * cap, axis=1)
            out[owner] += jnp.where(lane_part == part, wide, 0.0)


def merge(h_slot, p_slot, h_blocks, p_blocks, n_rows, cap):
    own_rows, n_local, b, _ = h_blocks.shape
    blocks = pl.BlockSpec((1, n_local, b, b), lambda i, *_: (i, 0, 0, 0))
    merged = pl.BlockSpec((n_rows, b, cap * b), lambda i, *_: (0, i, 0))
    shape = jax.ShapeDtypeStruct((n_rows, own_rows * b, cap * b), jnp.float32)
    return pl.pallas_call(
        functools.partial(merge_kernel, cap),
        out_shape=(shape, shape),
        grid_spec=pltpu.PrefetchScalarGridSpec(
            num_scalar_prefetch=2, grid=(own_rows,), in_specs=[blocks, blocks], out_specs=[merged, merged]
        ),
        name="merge",
    )(h_slot, p_slot, h_blocks, p_blocks)


def split(x):
    high = x.astype(jnp.bfloat16)
    return high, (x - high.astype(jnp.float32)).astype(jnp.bfloat16)


def product_kernel(
    n_rows, n_cols, cap, b,
    dh, dp, fetch, panel, out,
    lists, wanted, rs_buf, y_send, y_recv, total, from_sib, d_high, d_low,
    packed, slots, b_both, x_buf,
    list_s, list_r, list_l, rs_s, rs_r, y_s, y_r, ag_s, ag_r, slot_s, slot_r,
):
    me, c = lax.axis_index("rows"), lax.axis_index("cols")
    core = lax.rem(c, 2)
    sibling = c + 1 - 2 * core
    across = lax.rem(c + 2, n_cols)
    per_half = n_rows // 2
    mine, theirs = core * per_half, (1 - core) * per_half
    halves = panel.shape[2] // LANES
    depth = cap * b
    rows_all = panel.shape[0] * b

    def right(k):
        return lax.rem(me + k, n_rows)

    def left(k):
        return lax.rem(me + n_rows - k, n_rows)

    barrier = pltpu.get_barrier_semaphore()
    for k in range(1, n_rows):
        pl.semaphore_signal(barrier, inc=1, device_id={"rows": right(k)}, device_id_type=MESH)
    for other in (sibling, across):
        pl.semaphore_signal(barrier, inc=1, device_id={"cols": other}, device_id_type=MESH)
    pl.semaphore_wait(barrier, n_rows + 1)

    def remote(src, dst, s, r, where):
        return pltpu.make_async_remote_copy(
            src_ref=src, dst_ref=dst, send_sem=s, recv_sem=r, device_id=where, device_id_type=MESH
        )

    started = []

    def start(copy):
        copy.start()
        started.append(copy)
        return copy

    def scatter(q, source):
        return [
            start(remote(source.at[theirs + t], rs_buf.at[q, t], rs_s.at[q, t], rs_r.at[q, t], {"cols": sibling}))
            for t in range(per_half)
        ]

    def cross(q, t):
        return start(remote(y_send.at[q, t], y_recv.at[q, t], y_s.at[q, t], y_r.at[q, t], {"cols": across}))

    def hand_over(q, t):
        return start(remote(total.at[q, t], from_sib.at[q, t], ag_s.at[q, t], ag_r.at[q, t], {"cols": sibling}))

    def columns_of(owner):
        return pl.ds(pl.multiple_of(owner * depth, depth), depth)

    def keep(owner, value):
        high, low = split(value)
        d_high[:, columns_of(owner)] = high
        d_low[:, columns_of(owner)] = low

    def keep_slots(h, owner, value):
        high, low = split(value)
        b_both[h, columns_of(owner), :LANES] = high
        b_both[h, columns_of(owner), LANES:] = low

    def multiply_half(h, store):
        tile = cap * b
        right_side = b_both[h]

        def step(i, carry):
            rows = pl.ds(pl.multiple_of(i * tile, tile), tile)
            both = jnp.dot(d_high[rows, :], right_side, preferred_element_type=jnp.float32)
            low = jnp.dot(d_low[rows, :], right_side[:, :LANES], preferred_element_type=jnp.float32)
            store(i, rows, both[:, :LANES] + (both[:, LANES:] + low))
            return carry

        lax.fori_loop(0, rows_all // tile, step, 0)

    list_copies = [
        start(remote(fetch.at[right(k)], lists.at[me], list_s.at[k], list_r.at[k], {"rows": right(k)}))
        for k in range(1, n_rows)
    ]
    h_scatter = scatter(0, dh)
    h_cross, p_cross = [], []
    for t in range(per_half):
        h_scatter[t].wait_recv()
        y_send[0, t] = dh[mine + t] + rs_buf[0, t]
        h_cross.append(cross(0, t))
    p_scatter = scatter(1, dp)
    for copy in list_copies:
        copy.wait_recv()
    lists[me] = fetch[me]
    local = pltpu.make_async_copy(lists, wanted, list_l)
    local.start()
    local.wait()

    def pack(q, h, k, source):
        to = right(k)
        for e in range(cap):
            row = wanted[to, 0, q * cap + e]
            packed[q, h, k, e * b:(e + 1) * b, :] = source(h, row)

    def send_slots(q, h, k):
        return start(
            remote(packed.at[q, h, k], slots.at[q, h, k], slot_s.at[q, h, k], slot_r.at[q, h, k], {"rows": right(k)})
        )

    def panel_rows(h, row):
        return panel[row, :, h * LANES:(h + 1) * LANES]

    def x_rows(h, row):
        return x_buf[h, row]

    panel_copies = {}
    for h in range(halves):
        for k in range(1, n_rows):
            pack(0, h, k, panel_rows)
            panel_copies[h, k] = send_slots(0, h, k)
    for h in range(halves):
        pack(0, h, 0, panel_rows)
        keep_slots(h, me, packed[0, h, 0])

    for t in range(per_half):
        p_scatter[t].wait_recv()
        y_send[1, t] = dp[mine + t] + rs_buf[1, t]

    def finish(q, copies, after):
        handed = []
        for t in range(per_half):
            copies[t].wait_recv()
            total[q, t] = y_send[q, t] + y_recv[q, t]
            handed.append(hand_over(q, t))
            after(t)
            keep(mine + t, total[q, t])
        for t in range(per_half):
            handed[t].wait_recv()
            keep(theirs + t, from_sib[q, t])

    def start_p(t):
        if t >= per_half - 2:
            upto = per_half if t == per_half - 1 else 1
            while len(p_cross) < upto:
                p_cross.append(cross(1, len(p_cross)))

    finish(0, h_cross, start_p)

    x_copies = {}
    for h in range(halves):
        for k in range(1, n_rows):
            panel_copies[h, k].wait_recv()
            keep_slots(h, left(k), slots[0, h, k])

        def store_x(i, rows, value, h=h):
            for e in range(cap):
                x_buf[h, i * cap + e] = value[e * b:(e + 1) * b]

        multiply_half(h, store_x)
        for k in range(1, n_rows):
            pack(1, h, k, x_rows)
            x_copies[h, k] = send_slots(1, h, k)
    for h in range(halves):
        pack(1, h, 0, x_rows)
        keep_slots(h, me, packed[1, h, 0])

    finish(1, p_cross, lambda t: None)

    for h in range(halves):
        for k in range(1, n_rows):
            x_copies[h, k].wait_recv()
            keep_slots(h, left(k), slots[1, h, k])

        def store_w(i, rows, value, h=h):
            out[rows, h * LANES:(h + 1) * LANES] = value

        multiply_half(h, store_w)
    for copy in started:
        copy.wait_send()


def merged_body(n_rows, n_cols, h_blocks, p_blocks, h_fetch, p_fetch, h_slot, p_slot, p_panel):
    cap, b = h_fetch.shape[2], h_blocks.shape[2]
    rows_all, columns = p_panel.shape
    depth, per_half, halves = cap * b, n_rows // 2, columns // LANES
    dh, dp = merge(h_slot, p_slot, h_blocks, p_blocks, n_rows, cap)
    fetch = jnp.concatenate([h_fetch[0], p_fetch[0]], axis=1)
    fetch = jnp.pad(fetch, ((0, 0), (0, LANES - 2 * cap))).reshape(n_rows, 1, LANES)
    f32, bf16, dma = jnp.float32, jnp.bfloat16, pltpu.SemaphoreType.DMA
    exchanged = pltpu.VMEM((2, per_half, rows_all, depth), f32)
    vmem = pl.BlockSpec(memory_space=pltpu.VMEM)
    return pl.pallas_call(
        functools.partial(product_kernel, n_rows, n_cols, cap, b),
        out_shape=jax.ShapeDtypeStruct((rows_all, columns), f32),
        in_specs=[vmem] * 4,
        out_specs=vmem,
        scratch_shapes=[
            pltpu.VMEM((n_rows, 1, LANES), jnp.int32),
            pltpu.SMEM((n_rows, 1, LANES), jnp.int32),
            exchanged, exchanged, exchanged, exchanged, exchanged,
            pltpu.VMEM((rows_all, n_rows * depth), bf16),
            pltpu.VMEM((rows_all, n_rows * depth), bf16),
            pltpu.VMEM((2, halves, n_rows, depth, LANES), f32),
            pltpu.VMEM((2, halves, n_rows, depth, LANES), f32),
            pltpu.VMEM((halves, n_rows * depth, 2 * LANES), bf16),
            pltpu.VMEM((halves, rows_all // b, b, LANES), f32),
            dma((n_rows,)), dma((n_rows,)), dma,
            dma((2, per_half)), dma((2, per_half)),
            dma((2, per_half)), dma((2, per_half)),
            dma((2, per_half)), dma((2, per_half)),
            dma((2, halves, n_rows)), dma((2, halves, n_rows)),
        ],
        compiler_params=pltpu.CompilerParams(
            collective_id=0, has_side_effects=True, vmem_limit_bytes=48 * 1024 * 1024
        ),
        name="product",
    )(dh, dp, fetch, p_panel.reshape(-1, b, columns))


def solution(mesh):
    n_rows, n_cols = mesh.shape["rows"], mesh.shape["cols"]
    in_specs = (
        P("rows", "cols", None, None),
        P("rows", "cols", None, None),
        P("rows", None, None),
        P("rows", None, None),
        P("rows", None),
        P("rows", None),
        P("rows", "cols"),
    )
    out_specs = P("rows", "cols")

    def body(h_blocks, p_blocks, h_fetch, p_fetch, h_slot, p_slot, p_panel):
        cap, b = h_fetch.shape[2], h_blocks.shape[2]
        fits = n_cols == 4 and n_rows % 2 == 0 and cap * b == LANES and h_blocks.shape[0] % cap == 0 and p_panel.shape[1] % LANES == 0
        arguments = (h_blocks, p_blocks, h_fetch, p_fetch, h_slot, p_slot, p_panel)
        if fits and cap * n_rows <= h_slot.shape[1]:
            return merged_body(n_rows, n_cols, *arguments)
        return list_body(*arguments)

    return jax.shard_map(body, mesh=mesh, in_specs=in_specs, out_specs=out_specs, check_vma=False)
```

```python
import functools

import jax
import jax.numpy as jnp
from jax import lax
from jax.experimental import pallas as pl
from jax.experimental.pallas import tpu as pltpu
from jax.sharding import PartitionSpec as P

highest = lax.Precision.HIGHEST
MESH = pl.DeviceIdType.MESH
LANES = 128


def take_kernel(indices, slab, out):
    out[...] = slab[...]


def take_slabs(slabs, indices):
    _, b, columns = slabs.shape
    slab = (1, b, columns)
    taken = pl.pallas_call(
        take_kernel,
        out_shape=jax.ShapeDtypeStruct((indices.size, b, columns), slabs.dtype),
        grid_spec=pltpu.PrefetchScalarGridSpec(
            num_scalar_prefetch=1,
            grid=(indices.size,),
            in_specs=[pl.BlockSpec(slab, lambda i, wanted: (wanted[i], 0, 0))],
            out_specs=pl.BlockSpec(slab, lambda i, wanted: (i, 0, 0)),
        ),
        name="take_slabs",
    )(indices.reshape(-1), slabs)
    return taken.reshape(*indices.shape, b, columns)


def multiply(block_list, fetch_lists, slot_lists, panel_part):
    own_rows = block_list.shape[0]
    block_size = block_list.shape[2]
    columns = panel_part.shape[1]
    wanted = lax.all_to_all(fetch_lists[0], "rows", split_axis=0, concat_axis=0, tiled=True)
    stacked = panel_part.reshape(own_rows, block_size, columns)
    packed = take_slabs(stacked, wanted)
    arrived = lax.all_to_all(packed, "rows", split_axis=0, concat_axis=0, tiled=True)
    flattened = arrived.reshape(-1, block_size, columns)
    chosen = take_slabs(flattened, slot_lists)
    result = jnp.einsum("ijab,ijbc->iac", block_list, chosen, precision=highest)
    return result.reshape(own_rows * block_size, columns)


def list_body(h_blocks, p_blocks, h_fetch, p_fetch, h_slot, p_slot, p_panel):
    gathered = (
        lax.all_gather(h_blocks, "cols", axis=1, tiled=True),
        lax.all_gather(p_blocks, "cols", axis=1, tiled=True),
    )
    middle = multiply(gathered[0], h_fetch, h_slot, p_panel)
    return multiply(gathered[1], p_fetch, p_slot, middle)


def split(x):
    high = x.astype(jnp.bfloat16)
    return high, (x - high.astype(jnp.float32)).astype(jnp.bfloat16)


def product_kernel(
    n_rows, n_cols, cap, b,
    h_slot, p_slot, h_fetch, p_fetch, h_blocks, p_blocks, panel, out,
    blocks, merged, message, lists, wanted, rs_buf, y_send, y_recv, total, from_sib, d_high, d_low,
    packed, slots, b_both, x_buf,
    load_s, list_s, list_r, list_l, rs_s, rs_r, y_s, y_r, ag_s, ag_r, slot_s, slot_r,
):
    me, c = lax.axis_index("rows"), lax.axis_index("cols")
    core = lax.rem(c, 2)
    sibling = c + 1 - 2 * core
    across = lax.rem(c + 2, n_cols)
    per_half = n_rows // 2
    mine, theirs = core * per_half, (1 - core) * per_half
    halves = panel.shape[2] // LANES
    depth = cap * b
    rows_all = panel.shape[0] * b

    def right(k):
        return lax.rem(me + k, n_rows)

    def left(k):
        return lax.rem(me + n_rows - k, n_rows)

    loads = [pltpu.make_async_copy(source, blocks.at[q], load_s.at[q]) for q, source in enumerate((h_blocks, p_blocks))]
    for load in loads:
        load.start()
    slot_lists = (h_slot, p_slot)
    own_rows, n_local = blocks.shape[1:3]
    lane_part = lax.broadcasted_iota(jnp.int32, (8, depth), 1) // b

    def merge(q, first_owner):
        slot_list = slot_lists[q]

        def step(i, carry):
            sums = [jnp.zeros((b // 8, 8, depth), jnp.float32)] * per_half
            for j in range(n_local):
                slot = slot_list[i, c * n_local + j] - first_owner * cap
                block = blocks[q, i, j]
                wide = jnp.concatenate([block] * cap, axis=1).reshape(b // 8, 8, depth)
                for t in range(per_half):
                    named = (lane_part == slot - t * cap)[None]
                    sums[t] = sums[t] + jnp.where(named, wide, 0.0)
            rows = pl.ds(pl.multiple_of(i * b, b), b)
            for t in range(per_half):
                merged[q, first_owner + t, rows, :] = sums[t].reshape(b, depth)
            return carry

        lax.fori_loop(0, own_rows, step, 0)

    barrier = pltpu.get_barrier_semaphore()
    for k in range(1, n_rows):
        pl.semaphore_signal(barrier, inc=1, device_id={"rows": right(k)}, device_id_type=MESH)
    for other in (sibling, across):
        pl.semaphore_signal(barrier, inc=1, device_id={"cols": other}, device_id_type=MESH)
    lane = lax.broadcasted_iota(jnp.int32, (1, LANES), 1)
    for o in range(n_rows):
        row = jnp.zeros((1, LANES), jnp.int32)
        for q, fetch in enumerate((h_fetch, p_fetch)):
            for e in range(cap):
                row = jnp.where(lane == q * cap + e, fetch[0, e, o], row)
        message[o] = row
    loads[0].wait()
    merge(0, theirs)
    pl.semaphore_wait(barrier, n_rows + 1)

    def remote(src, dst, s, r, where):
        return pltpu.make_async_remote_copy(
            src_ref=src, dst_ref=dst, send_sem=s, recv_sem=r, device_id=where, device_id_type=MESH
        )

    started = []

    def start(copy):
        copy.start()
        started.append(copy)
        return copy

    def scatter(q):
        return [
            start(remote(merged.at[q, theirs + t], rs_buf.at[q, t], rs_s.at[q, t], rs_r.at[q, t], {"cols": sibling}))
            for t in range(per_half)
        ]

    def cross(q, t):
        return start(remote(y_send.at[q, t], y_recv.at[q, t], y_s.at[q, t], y_r.at[q, t], {"cols": across}))

    def hand_over(q, t):
        return start(remote(total.at[q, t], from_sib.at[q, t], ag_s.at[q, t], ag_r.at[q, t], {"cols": sibling}))

    def columns_of(owner):
        return pl.ds(pl.multiple_of(owner * depth, depth), depth)

    def keep(owner, value):
        high, low = split(value)
        d_high[:, columns_of(owner)] = high
        d_low[:, columns_of(owner)] = low

    def keep_slots(h, owner, value):
        high, low = split(value)
        b_both[h, columns_of(owner), :LANES] = high
        b_both[h, columns_of(owner), LANES:] = low

    def multiply_half(h, store):
        tile = cap * b
        right_side = b_both[h]

        def step(i, carry):
            rows = pl.ds(pl.multiple_of(i * tile, tile), tile)
            both = jnp.dot(d_high[rows, :], right_side, preferred_element_type=jnp.float32)
            low = jnp.dot(d_low[rows, :], right_side[:, :LANES], preferred_element_type=jnp.float32)
            store(i, rows, both[:, :LANES] + (both[:, LANES:] + low))
            return carry

        lax.fori_loop(0, rows_all // tile, step, 0)

    list_copies = [
        start(remote(message.at[right(k)], lists.at[me], list_s.at[k], list_r.at[k], {"rows": right(k)}))
        for k in range(1, n_rows)
    ]
    h_scatter = scatter(0)
    merge(0, mine)
    h_cross, p_cross = [], []
    for t in range(per_half):
        h_scatter[t].wait_recv()
        y_send[0, t] = merged[0, mine + t] + rs_buf[0, t]
        h_cross.append(cross(0, t))
    for copy in list_copies:
        copy.wait_recv()
    lists[me] = message[me]
    local = pltpu.make_async_copy(lists, wanted, list_l)
    local.start()
    local.wait()

    def pack(q, h, k, source):
        to = right(k)
        for e in range(cap):
            row = wanted[to, 0, q * cap + e]
            packed[q, h, k, e * b:(e + 1) * b, :] = source(h, row)

    def send_slots(q, h, k):
        return start(
            remote(packed.at[q, h, k], slots.at[q, h, k], slot_s.at[q, h, k], slot_r.at[q, h, k], {"rows": right(k)})
        )

    def panel_rows(h, row):
        return panel[row, :, h * LANES:(h + 1) * LANES]

    def x_rows(h, row):
        return x_buf[h, row]

    panel_copies = {}
    for h in range(halves):
        for k in range(1, n_rows):
            pack(0, h, k, panel_rows)
            panel_copies[h, k] = send_slots(0, h, k)
    for h in range(halves):
        pack(0, h, 0, panel_rows)
        keep_slots(h, me, packed[0, h, 0])

    loads[1].wait()
    merge(1, theirs)
    p_scatter = scatter(1)
    merge(1, mine)
    for t in range(per_half):
        p_scatter[t].wait_recv()
        y_send[1, t] = merged[1, mine + t] + rs_buf[1, t]

    def finish(q, copies, after):
        handed = []
        for t in range(per_half):
            copies[t].wait_recv()
            total[q, t] = y_send[q, t] + y_recv[q, t]
            handed.append(hand_over(q, t))
            after(t)
            keep(mine + t, total[q, t])
        for t in range(per_half):
            handed[t].wait_recv()
            keep(theirs + t, from_sib[q, t])

    def start_p(t):
        if t >= per_half - 2:
            upto = per_half if t == per_half - 1 else 1
            while len(p_cross) < upto:
                p_cross.append(cross(1, len(p_cross)))

    finish(0, h_cross, start_p)

    x_copies = {}
    for h in range(halves):
        for k in range(1, n_rows):
            panel_copies[h, k].wait_recv()
            keep_slots(h, left(k), slots[0, h, k])

        def store_x(i, rows, value, h=h):
            for e in range(cap):
                x_buf[h, i * cap + e] = value[e * b:(e + 1) * b]

        multiply_half(h, store_x)
        for k in range(1, n_rows):
            pack(1, h, k, x_rows)
            x_copies[h, k] = send_slots(1, h, k)
    for h in range(halves):
        pack(1, h, 0, x_rows)
        keep_slots(h, me, packed[1, h, 0])

    finish(1, p_cross, lambda t: None)

    for h in range(halves):
        for k in range(1, n_rows):
            x_copies[h, k].wait_recv()
            keep_slots(h, left(k), slots[1, h, k])

        def store_w(i, rows, value, h=h):
            out[rows, h * LANES:(h + 1) * LANES] = value

        multiply_half(h, store_w)
    for copy in started:
        copy.wait_send()


def merged_body(n_rows, n_cols, h_blocks, p_blocks, h_fetch, p_fetch, h_slot, p_slot, p_panel):
    cap, b = h_fetch.shape[2], h_blocks.shape[2]
    rows_all, columns = p_panel.shape
    depth, per_half, halves = cap * b, n_rows // 2, columns // LANES
    f32, bf16, dma = jnp.float32, jnp.bfloat16, pltpu.SemaphoreType.DMA
    exchanged = pltpu.VMEM((2, per_half, rows_all, depth), f32)
    slots_and_lists = (h_slot, p_slot, jnp.swapaxes(h_fetch, 1, 2), jnp.swapaxes(p_fetch, 1, 2))
    vmem, smem = pl.BlockSpec(memory_space=pltpu.VMEM), pl.BlockSpec(memory_space=pltpu.SMEM)
    return pl.pallas_call(
        functools.partial(product_kernel, n_rows, n_cols, cap, b),
        out_shape=jax.ShapeDtypeStruct((rows_all, columns), f32),
        in_specs=[smem] * 4 + [pl.BlockSpec(memory_space=pltpu.HBM)] * 2 + [vmem],
        out_specs=vmem,
        scratch_shapes=[
            pltpu.VMEM((2, *h_blocks.shape), f32),
            pltpu.VMEM((2, n_rows, rows_all, depth), f32),
            pltpu.VMEM((n_rows, 1, LANES), jnp.int32),
            pltpu.VMEM((n_rows, 1, LANES), jnp.int32),
            pltpu.SMEM((n_rows, 1, LANES), jnp.int32),
            exchanged, exchanged, exchanged, exchanged, exchanged,
            pltpu.VMEM((rows_all, n_rows * depth), bf16),
            pltpu.VMEM((rows_all, n_rows * depth), bf16),
            pltpu.VMEM((2, halves, n_rows, depth, LANES), f32),
            pltpu.VMEM((2, halves, n_rows, depth, LANES), f32),
            pltpu.VMEM((halves, n_rows * depth, 2 * LANES), bf16),
            pltpu.VMEM((halves, rows_all // b, b, LANES), f32),
            dma((2,)), dma((n_rows,)), dma((n_rows,)), dma,
            dma((2, per_half)), dma((2, per_half)),
            dma((2, per_half)), dma((2, per_half)),
            dma((2, per_half)), dma((2, per_half)),
            dma((2, halves, n_rows)), dma((2, halves, n_rows)),
        ],
        compiler_params=pltpu.CompilerParams(
            collective_id=0, has_side_effects=True, vmem_limit_bytes=48 * 1024 * 1024
        ),
        name="product",
    )(*slots_and_lists, h_blocks, p_blocks, p_panel.reshape(-1, b, columns))


def solution(mesh):
    n_rows, n_cols = mesh.shape["rows"], mesh.shape["cols"]
    in_specs = (
        P("rows", "cols", None, None),
        P("rows", "cols", None, None),
        P("rows", None, None),
        P("rows", None, None),
        P("rows", None),
        P("rows", None),
        P("rows", "cols"),
    )
    out_specs = P("rows", "cols")

    def body(h_blocks, p_blocks, h_fetch, p_fetch, h_slot, p_slot, p_panel):
        cap, b = h_fetch.shape[2], h_blocks.shape[2]
        fits = n_cols == 4 and n_rows % 2 == 0 and cap * b == LANES and h_blocks.shape[0] % cap == 0 and p_panel.shape[1] % LANES == 0
        arguments = (h_blocks, p_blocks, h_fetch, p_fetch, h_slot, p_slot, p_panel)
        if fits and cap * n_rows <= h_slot.shape[1]:
            return merged_body(n_rows, n_cols, *arguments)
        return list_body(*arguments)

    return jax.shard_map(body, mesh=mesh, in_specs=in_specs, out_specs=out_specs, check_vma=False)
```

```python
import functools

import jax
import jax.numpy as jnp
from jax import lax
from jax.experimental import pallas as pl
from jax.experimental.pallas import tpu as pltpu
from jax.sharding import PartitionSpec as P

highest = lax.Precision.HIGHEST
MESH = pl.DeviceIdType.MESH
LANES = 128


def take_kernel(indices, slab, out):
    out[...] = slab[...]


def take_slabs(slabs, indices):
    _, b, columns = slabs.shape
    slab = (1, b, columns)
    taken = pl.pallas_call(
        take_kernel,
        out_shape=jax.ShapeDtypeStruct((indices.size, b, columns), slabs.dtype),
        grid_spec=pltpu.PrefetchScalarGridSpec(
            num_scalar_prefetch=1,
            grid=(indices.size,),
            in_specs=[pl.BlockSpec(slab, lambda i, wanted: (wanted[i], 0, 0))],
            out_specs=pl.BlockSpec(slab, lambda i, wanted: (i, 0, 0)),
        ),
        name="take_slabs",
    )(indices.reshape(-1), slabs)
    return taken.reshape(*indices.shape, b, columns)


def multiply(block_list, fetch_lists, slot_lists, panel_part):
    own_rows = block_list.shape[0]
    block_size = block_list.shape[2]
    columns = panel_part.shape[1]
    wanted = lax.all_to_all(fetch_lists[0], "rows", split_axis=0, concat_axis=0, tiled=True)
    stacked = panel_part.reshape(own_rows, block_size, columns)
    packed = take_slabs(stacked, wanted)
    arrived = lax.all_to_all(packed, "rows", split_axis=0, concat_axis=0, tiled=True)
    flattened = arrived.reshape(-1, block_size, columns)
    chosen = take_slabs(flattened, slot_lists)
    result = jnp.einsum("ijab,ijbc->iac", block_list, chosen, precision=highest)
    return result.reshape(own_rows * block_size, columns)


def list_body(h_blocks, p_blocks, h_fetch, p_fetch, h_slot, p_slot, p_panel):
    gathered = (
        lax.all_gather(h_blocks, "cols", axis=1, tiled=True),
        lax.all_gather(p_blocks, "cols", axis=1, tiled=True),
    )
    middle = multiply(gathered[0], h_fetch, h_slot, p_panel)
    return multiply(gathered[1], p_fetch, p_slot, middle)


def split(x):
    high = x.astype(jnp.bfloat16)
    return high, (x - high.astype(jnp.float32)).astype(jnp.bfloat16)


def product_kernel(
    n_rows, n_cols, cap, b,
    h_slot, p_slot, h_fetch, p_fetch, h_blocks, p_blocks, panel, out,
    blocks, merged, message, lists, wanted, rs_buf, y_send, y_recv, total, from_sib, d_high, d_low,
    packed, slots, b_high, b_low, x_buf,
    load_s, list_s, list_r, list_l, rs_s, rs_r, y_s, y_r, ag_s, ag_r, slot_s, slot_r,
):
    me, c = lax.axis_index("rows"), lax.axis_index("cols")
    core = lax.rem(c, 2)
    sibling = c + 1 - 2 * core
    across = lax.rem(c + 2, n_cols)
    per_half = n_rows // 2
    mine, theirs = core * per_half, (1 - core) * per_half
    halves = panel.shape[2] // LANES
    depth = cap * b
    rows_all = panel.shape[0] * b

    def right(k):
        return lax.rem(me + k, n_rows)

    def left(k):
        return lax.rem(me + n_rows - k, n_rows)

    tile = cap * b
    tiles = rows_all // tile

    def load(q, t):
        some = pl.ds(t * cap, cap)
        return pltpu.make_async_copy((h_blocks, p_blocks)[q].at[some], blocks.at[q, some], load_s.at[q, t])

    for q in range(2):
        for t in range(tiles):
            load(q, t).start()
    slot_lists = (h_slot, p_slot)
    own_rows, n_local = blocks.shape[1:3]
    lane_part = lax.broadcasted_iota(jnp.int32, (8, depth), 1) // b

    def merge(q, first_owner, start_row, end_row):
        slot_list = slot_lists[q]

        def step(i, carry):
            sums = [jnp.zeros((b // 8, 8, depth), jnp.float32)] * per_half
            for j in range(n_local):
                slot = slot_list[i, c * n_local + j] - first_owner * cap
                block = blocks[q, i, j]
                wide = jnp.concatenate([block] * cap, axis=1).reshape(b // 8, 8, depth)
                for t in range(per_half):
                    named = (lane_part == slot - t * cap)[None]
                    sums[t] = sums[t] + jnp.where(named, wide, 0.0)
            rows = pl.ds(pl.multiple_of(i * b, b), b)
            for t in range(per_half):
                merged[q, first_owner + t, rows, :] = sums[t].reshape(b, depth)
            return carry

        lax.fori_loop(start_row, end_row, step, 0)

    barrier = pltpu.get_barrier_semaphore()
    for k in range(1, n_rows):
        pl.semaphore_signal(barrier, inc=1, device_id={"rows": right(k)}, device_id_type=MESH)
    for other in (sibling, across):
        pl.semaphore_signal(barrier, inc=1, device_id={"cols": other}, device_id_type=MESH)
    lane = lax.broadcasted_iota(jnp.int32, (1, LANES), 1)
    for o in range(n_rows):
        row = jnp.zeros((1, LANES), jnp.int32)
        for q, fetch in enumerate((h_fetch, p_fetch)):
            for e in range(cap):
                row = jnp.where(lane == q * cap + e, fetch[0, e, o], row)
        message[o] = row
    for t in range(tiles):
        load(0, t).wait()
    merge(0, theirs, 0, own_rows)
    pl.semaphore_wait(barrier, n_rows + 1)

    def remote(src, dst, s, r, where):
        return pltpu.make_async_remote_copy(
            src_ref=src, dst_ref=dst, send_sem=s, recv_sem=r, device_id=where, device_id_type=MESH
        )

    started = []

    def start(copy):
        copy.start()
        started.append(copy)
        return copy

    def rows_of(t):
        return pl.ds(t * tile, tile)

    def scatter(q):
        source = merged.at[q, pl.ds(theirs, per_half)]
        return [
            start(remote(source.at[:, rows_of(t)], rs_buf.at[q, :, rows_of(t)], rs_s.at[q, t], rs_r.at[q, t], {"cols": sibling}))
            for t in range(tiles)
        ]

    def add_cores(q, t, arriving):
        arriving.wait_recv()
        y_send[q, :, rows_of(t)] = merged[q, pl.ds(mine, per_half), rows_of(t)] + rs_buf[q, :, rows_of(t)]

    def cross(q, t):
        part = (q, slice(None), rows_of(t))
        return start(remote(y_send.at[part], y_recv.at[part], y_s.at[q, t], y_r.at[q, t], {"cols": across}))

    def hand_over(q, t):
        part = (q, slice(None), rows_of(t))
        return start(remote(total.at[part], from_sib.at[part], ag_s.at[q, t], ag_r.at[q, t], {"cols": sibling}))

    def columns_of(owner):
        return pl.ds(pl.multiple_of(owner * depth, depth), depth)

    def keep(first_owner, t, value):
        for o in range(per_half):
            high, low = split(value[o])
            d_high[rows_of(t), columns_of(first_owner + o)] = high
            d_low[rows_of(t), columns_of(first_owner + o)] = low

    def keep_slots(h, owner, value):
        high, low = split(value)
        b_high[columns_of(owner), h * LANES:(h + 1) * LANES] = high
        b_low[columns_of(owner), h * LANES:(h + 1) * LANES] = low

    def multiply_tile(rows, lanes):
        f32 = jnp.float32
        high = jnp.dot(d_high[rows, :], b_high[:, lanes], preferred_element_type=f32)
        cross_terms = jnp.dot(d_high[rows, :], b_low[:, lanes], preferred_element_type=f32)
        return high + (cross_terms + jnp.dot(d_low[rows, :], b_high[:, lanes], preferred_element_type=f32))

    list_copies = [
        start(remote(message.at[right(k)], lists.at[me], list_s.at[k], list_r.at[k], {"rows": right(k)}))
        for k in range(1, n_rows)
    ]
    h_scatter = scatter(0)
    h_cross, p_cross = [], []
    for t in range(tiles):
        merge(0, mine, t * cap, (t + 1) * cap)
        add_cores(0, t, h_scatter[t])
        h_cross.append(cross(0, t))
    for copy in list_copies:
        copy.wait_recv()
    lists[me] = message[me]
    local = pltpu.make_async_copy(lists, wanted, list_l)
    local.start()
    local.wait()

    def pack(q, h, k, source):
        to = right(k)
        for e in range(cap):
            row = wanted[to, 0, q * cap + e]
            packed[q, h, k, e * b:(e + 1) * b, :] = source(h, row)

    def send_slots(q, h, k):
        return start(
            remote(packed.at[q, h, k], slots.at[q, h, k], slot_s.at[q, h, k], slot_r.at[q, h, k], {"rows": right(k)})
        )

    def panel_rows(h, row):
        return panel[row, :, h * LANES:(h + 1) * LANES]

    def x_rows(h, row):
        return x_buf[h, row]

    panel_copies = {}
    for h in range(halves):
        for k in range(1, n_rows):
            pack(0, h, k, panel_rows)
            panel_copies[h, k] = send_slots(0, h, k)
    for h in range(halves):
        pack(0, h, 0, panel_rows)
        keep_slots(h, me, packed[0, h, 0])

    for t in range(tiles):
        load(1, t).wait()
    merge(1, theirs, 0, own_rows)
    p_scatter = scatter(1)
    merge(1, mine, 0, own_rows)
    for t in range(tiles):
        add_cores(1, t, p_scatter[t])

    def arrive(q, t, crossing):
        crossing.wait_recv()
        part = (q, slice(None), rows_of(t))
        total[part] = y_send[part] + y_recv[part]
        handed = hand_over(q, t)
        return handed

    def take_sibling(q, t, handed):
        handed.wait_recv()
        keep(theirs, t, from_sib[q, :, rows_of(t)])

    handed = []
    for t in range(tiles):
        handed.append(arrive(0, t, h_cross[t]))
        if t == tiles - 2:
            p_cross.append(cross(1, 0))
        if t == tiles - 1:
            p_cross += [cross(1, u) for u in range(len(p_cross), tiles)]
        keep(mine, t, total[0, :, rows_of(t)])
        if t > 0:
            take_sibling(0, t - 1, handed[t - 1])

    for h in range(halves):
        for k in range(1, n_rows):
            panel_copies[h, k].wait_recv()
            keep_slots(h, left(k), slots[0, h, k])
    for t in range(tiles):
        if t == tiles - 1:
            take_sibling(0, t, handed[t])
        value = multiply_tile(rows_of(t), slice(None))
        for e in range(cap):
            for h in range(halves):
                x_buf[h, t * cap + e] = value[e * b:(e + 1) * b, h * LANES:(h + 1) * LANES]
    x_copies = {}
    for h in range(halves):
        for k in range(1, n_rows):
            pack(1, h, k, x_rows)
            x_copies[h, k] = send_slots(1, h, k)
    for h in range(halves):
        pack(1, h, 0, x_rows)
        keep_slots(h, me, packed[1, h, 0])

    handed = []
    for t in range(tiles):
        handed.append(arrive(1, t, p_cross[t]))
        keep(mine, t, total[1, :, rows_of(t)])
    for t in range(tiles):
        take_sibling(1, t, handed[t])

    for h in range(halves):
        lanes = slice(h * LANES, (h + 1) * LANES)
        for k in range(1, n_rows):
            x_copies[h, k].wait_recv()
            keep_slots(h, left(k), slots[1, h, k])
        for t in range(tiles):
            out[rows_of(t), lanes] = multiply_tile(rows_of(t), lanes)
    for copy in started:
        copy.wait_send()


def merged_body(n_rows, n_cols, h_blocks, p_blocks, h_fetch, p_fetch, h_slot, p_slot, p_panel):
    cap, b = h_fetch.shape[2], h_blocks.shape[2]
    rows_all, columns = p_panel.shape
    depth, per_half, halves = cap * b, n_rows // 2, columns // LANES
    tiles = rows_all // depth
    f32, bf16, dma = jnp.float32, jnp.bfloat16, pltpu.SemaphoreType.DMA
    exchanged = pltpu.VMEM((2, per_half, rows_all, depth), f32)
    slots_and_lists = (h_slot, p_slot, jnp.swapaxes(h_fetch, 1, 2), jnp.swapaxes(p_fetch, 1, 2))
    vmem, smem = pl.BlockSpec(memory_space=pltpu.VMEM), pl.BlockSpec(memory_space=pltpu.SMEM)
    return pl.pallas_call(
        functools.partial(product_kernel, n_rows, n_cols, cap, b),
        out_shape=jax.ShapeDtypeStruct((rows_all, columns), f32),
        in_specs=[smem] * 4 + [pl.BlockSpec(memory_space=pltpu.HBM)] * 2 + [vmem],
        out_specs=vmem,
        scratch_shapes=[
            pltpu.VMEM((2, *h_blocks.shape), f32),
            pltpu.VMEM((2, n_rows, rows_all, depth), f32),
            pltpu.VMEM((n_rows, 1, LANES), jnp.int32),
            pltpu.VMEM((n_rows, 1, LANES), jnp.int32),
            pltpu.SMEM((n_rows, 1, LANES), jnp.int32),
            exchanged, exchanged, exchanged, exchanged, exchanged,
            pltpu.VMEM((rows_all, n_rows * depth), bf16),
            pltpu.VMEM((rows_all, n_rows * depth), bf16),
            pltpu.VMEM((2, halves, n_rows, depth, LANES), f32),
            pltpu.VMEM((2, halves, n_rows, depth, LANES), f32),
            pltpu.VMEM((n_rows * depth, columns), bf16),
            pltpu.VMEM((n_rows * depth, columns), bf16),
            pltpu.VMEM((halves, rows_all // b, b, LANES), f32),
            dma((2, tiles)), dma((n_rows,)), dma((n_rows,)), dma,
            dma((2, tiles)), dma((2, tiles)),
            dma((2, tiles)), dma((2, tiles)),
            dma((2, tiles)), dma((2, tiles)),
            dma((2, halves, n_rows)), dma((2, halves, n_rows)),
        ],
        compiler_params=pltpu.CompilerParams(
            collective_id=0, has_side_effects=True, vmem_limit_bytes=58 * 1024 * 1024
        ),
        name="product",
    )(*slots_and_lists, h_blocks, p_blocks, p_panel.reshape(-1, b, columns))


def solution(mesh):
    n_rows, n_cols = mesh.shape["rows"], mesh.shape["cols"]
    in_specs = (
        P("rows", "cols", None, None),
        P("rows", "cols", None, None),
        P("rows", None, None),
        P("rows", None, None),
        P("rows", None),
        P("rows", None),
        P("rows", "cols"),
    )
    out_specs = P("rows", "cols")

    def body(h_blocks, p_blocks, h_fetch, p_fetch, h_slot, p_slot, p_panel):
        cap, b = h_fetch.shape[2], h_blocks.shape[2]
        fits = n_cols == 4 and n_rows % 2 == 0 and cap * b == LANES and h_blocks.shape[0] % cap == 0 and p_panel.shape[1] % LANES == 0
        arguments = (h_blocks, p_blocks, h_fetch, p_fetch, h_slot, p_slot, p_panel)
        if fits and cap * n_rows <= h_slot.shape[1]:
            return merged_body(n_rows, n_cols, *arguments)
        return list_body(*arguments)

    return jax.shard_map(body, mesh=mesh, in_specs=in_specs, out_specs=out_specs, check_vma=False)
```

```python
import functools

import jax
import jax.numpy as jnp
from jax import lax
from jax.experimental import pallas as pl
from jax.experimental.pallas import tpu as pltpu
from jax.sharding import PartitionSpec as P

highest = lax.Precision.HIGHEST
MESH = pl.DeviceIdType.MESH
LANES = 128


def take_kernel(indices, slab, out):
    out[...] = slab[...]


def take_slabs(slabs, indices):
    _, b, columns = slabs.shape
    slab = (1, b, columns)
    taken = pl.pallas_call(
        take_kernel,
        out_shape=jax.ShapeDtypeStruct((indices.size, b, columns), slabs.dtype),
        grid_spec=pltpu.PrefetchScalarGridSpec(
            num_scalar_prefetch=1,
            grid=(indices.size,),
            in_specs=[pl.BlockSpec(slab, lambda i, wanted: (wanted[i], 0, 0))],
            out_specs=pl.BlockSpec(slab, lambda i, wanted: (i, 0, 0)),
        ),
        name="take_slabs",
    )(indices.reshape(-1), slabs)
    return taken.reshape(*indices.shape, b, columns)


def multiply(block_list, fetch_lists, slot_lists, panel_part):
    own_rows = block_list.shape[0]
    block_size = block_list.shape[2]
    columns = panel_part.shape[1]
    wanted = lax.all_to_all(fetch_lists[0], "rows", split_axis=0, concat_axis=0, tiled=True)
    stacked = panel_part.reshape(own_rows, block_size, columns)
    packed = take_slabs(stacked, wanted)
    arrived = lax.all_to_all(packed, "rows", split_axis=0, concat_axis=0, tiled=True)
    flattened = arrived.reshape(-1, block_size, columns)
    chosen = take_slabs(flattened, slot_lists)
    result = jnp.einsum("ijab,ijbc->iac", block_list, chosen, precision=highest)
    return result.reshape(own_rows * block_size, columns)


def list_body(h_blocks, p_blocks, h_fetch, p_fetch, h_slot, p_slot, p_panel):
    gathered = (
        lax.all_gather(h_blocks, "cols", axis=1, tiled=True),
        lax.all_gather(p_blocks, "cols", axis=1, tiled=True),
    )
    middle = multiply(gathered[0], h_fetch, h_slot, p_panel)
    return multiply(gathered[1], p_fetch, p_slot, middle)


def split(x):
    high = x.astype(jnp.bfloat16)
    return high, (x - high.astype(jnp.float32)).astype(jnp.bfloat16)


def product_kernel(
    n_rows, n_cols, cap, b,
    h_slot, p_slot, h_fetch, p_fetch, h_blocks, p_blocks, panel, out,
    blocks, merged, message, lists, wanted, rs_buf, y_send, y_recv, total, from_sib, d_high, d_low,
    packed, slots, b_high, b_low, x_buf,
    load_s, list_s, list_r, list_l, rs_s, rs_r, y_s, y_r, ag_s, ag_r, slot_s, slot_r,
):
    me, c = lax.axis_index("rows"), lax.axis_index("cols")
    core = lax.rem(c, 2)
    sibling = c + 1 - 2 * core
    across = lax.rem(c + 2, n_cols)
    per_half = n_rows // 2
    mine, theirs = core * per_half, (1 - core) * per_half
    halves = panel.shape[2] // LANES
    depth = cap * b
    rows_all = panel.shape[0] * b

    def right(k):
        return lax.rem(me + k, n_rows)

    def left(k):
        return lax.rem(me + n_rows - k, n_rows)

    tile = cap * b
    tiles = rows_all // tile

    def load(q, t):
        some = pl.ds(t * cap, cap)
        return pltpu.make_async_copy((h_blocks, p_blocks)[q].at[some], blocks.at[q, some], load_s.at[q, t])

    for t in range(tiles):
        load(0, t).start()
    slot_lists = (h_slot, p_slot)
    own_rows, n_local = blocks.shape[1:3]
    lane_part = lax.broadcasted_iota(jnp.int32, (8, depth), 1) // b

    def merge(q, first_owner, start_row, end_row):
        slot_list = slot_lists[q]

        def step(i, carry):
            sums = [jnp.zeros((b // 8, 8, depth), jnp.float32)] * per_half
            for j in range(n_local):
                slot = slot_list[i, c * n_local + j] - first_owner * cap
                block = blocks[q, i, j]
                wide = jnp.concatenate([block] * cap, axis=1).reshape(b // 8, 8, depth)
                for t in range(per_half):
                    named = (lane_part == slot - t * cap)[None]
                    sums[t] = sums[t] + jnp.where(named, wide, 0.0)
            rows = pl.ds(pl.multiple_of(i * b, b), b)
            for t in range(per_half):
                merged[q, first_owner + t, rows, :] = sums[t].reshape(b, depth)
            return carry

        lax.fori_loop(start_row, end_row, step, 0)

    barrier = pltpu.get_barrier_semaphore()
    for k in range(1, n_rows):
        pl.semaphore_signal(barrier, inc=1, device_id={"rows": right(k)}, device_id_type=MESH)
    for other in (sibling, across):
        pl.semaphore_signal(barrier, inc=1, device_id={"cols": other}, device_id_type=MESH)
    lane = lax.broadcasted_iota(jnp.int32, (1, LANES), 1)
    for o in range(n_rows):
        row = jnp.zeros((1, LANES), jnp.int32)
        for q, fetch in enumerate((h_fetch, p_fetch)):
            for e in range(cap):
                row = jnp.where(lane == q * cap + e, fetch[0, e, o], row)
        message[o] = row
    load(0, 0).wait()
    merge(0, theirs, 0, cap)
    pl.semaphore_wait(barrier, n_rows + 1)

    def remote(src, dst, s, r, where):
        return pltpu.make_async_remote_copy(
            src_ref=src, dst_ref=dst, send_sem=s, recv_sem=r, device_id=where, device_id_type=MESH
        )

    started = []

    def start(copy):
        copy.start()
        started.append(copy)
        return copy

    def rows_of(t):
        return pl.ds(t * tile, tile)

    def scatter(q, t):
        source = merged.at[q, pl.ds(theirs, per_half)]
        return start(
            remote(source.at[:, rows_of(t)], rs_buf.at[q, :, rows_of(t)], rs_s.at[q, t], rs_r.at[q, t], {"cols": sibling})
        )

    def add_cores(q, t, arriving):
        arriving.wait_recv()
        y_send[q, :, rows_of(t)] = merged[q, pl.ds(mine, per_half), rows_of(t)] + rs_buf[q, :, rows_of(t)]

    def cross(q, t):
        part = (q, slice(None), rows_of(t))
        return start(remote(y_send.at[part], y_recv.at[part], y_s.at[q, t], y_r.at[q, t], {"cols": across}))

    def hand_over(q, t):
        part = (q, slice(None), rows_of(t))
        return start(remote(total.at[part], from_sib.at[part], ag_s.at[q, t], ag_r.at[q, t], {"cols": sibling}))

    def columns_of(owner):
        return pl.ds(pl.multiple_of(owner * depth, depth), depth)

    def keep(first_owner, t, value):
        for o in range(per_half):
            high, low = split(value[o])
            d_high[rows_of(t), columns_of(first_owner + o)] = high
            d_low[rows_of(t), columns_of(first_owner + o)] = low

    def keep_slots(h, owner, value):
        high, low = split(value)
        b_high[columns_of(owner), h * LANES:(h + 1) * LANES] = high
        b_low[columns_of(owner), h * LANES:(h + 1) * LANES] = low

    def multiply_tile(rows, lanes):
        f32 = jnp.float32
        high = jnp.dot(d_high[rows, :], b_high[:, lanes], preferred_element_type=f32)
        cross_terms = jnp.dot(d_high[rows, :], b_low[:, lanes], preferred_element_type=f32)
        return high + (cross_terms + jnp.dot(d_low[rows, :], b_high[:, lanes], preferred_element_type=f32))

    list_copies = [
        start(remote(message.at[right(k)], lists.at[me], list_s.at[k], list_r.at[k], {"rows": right(k)}))
        for k in range(1, n_rows)
    ]
    h_scatter = [scatter(0, 0)]
    for t in range(1, tiles):
        load(0, t).wait()
        merge(0, theirs, t * cap, (t + 1) * cap)
        h_scatter.append(scatter(0, t))
    for t in range(tiles):
        load(1, t).start()
    h_cross, p_cross = [], []
    for t in range(tiles):
        merge(0, mine, t * cap, (t + 1) * cap)
        add_cores(0, t, h_scatter[t])
        h_cross.append(cross(0, t))
    for copy in list_copies:
        copy.wait_recv()
    lists[me] = message[me]
    local = pltpu.make_async_copy(lists, wanted, list_l)
    local.start()
    local.wait()

    def pack(q, h, k, source):
        to = right(k)
        for e in range(cap):
            row = wanted[to, 0, q * cap + e]
            packed[q, h, k, e * b:(e + 1) * b, :] = source(h, row)

    def send_slots(q, h, k):
        return start(
            remote(packed.at[q, h, k], slots.at[q, h, k], slot_s.at[q, h, k], slot_r.at[q, h, k], {"rows": right(k)})
        )

    def panel_rows(h, row):
        return panel[row, :, h * LANES:(h + 1) * LANES]

    def x_rows(h, row):
        return x_buf[h, row]

    panel_copies = {}
    for h in range(halves):
        for k in range(1, n_rows):
            pack(0, h, k, panel_rows)
            panel_copies[h, k] = send_slots(0, h, k)
    for h in range(halves):
        pack(0, h, 0, panel_rows)
        keep_slots(h, me, packed[0, h, 0])

    for t in range(tiles):
        load(1, t).wait()
    merge(1, theirs, 0, own_rows)
    p_scatter = [scatter(1, t) for t in range(tiles)]
    merge(1, mine, 0, own_rows)
    for t in range(tiles):
        add_cores(1, t, p_scatter[t])

    def arrive(q, t, crossing):
        crossing.wait_recv()
        part = (q, slice(None), rows_of(t))
        total[part] = y_send[part] + y_recv[part]
        handed = hand_over(q, t)
        return handed

    def take_sibling(q, t, handed):
        handed.wait_recv()
        keep(theirs, t, from_sib[q, :, rows_of(t)])

    handed = []
    for t in range(tiles):
        handed.append(arrive(0, t, h_cross[t]))
        if t == tiles - 2:
            p_cross.append(cross(1, 0))
        if t == tiles - 1:
            p_cross += [cross(1, u) for u in range(len(p_cross), tiles)]
        keep(mine, t, total[0, :, rows_of(t)])
        if t > 0:
            take_sibling(0, t - 1, handed[t - 1])

    for h in range(halves):
        for k in range(1, n_rows):
            panel_copies[h, k].wait_recv()
            keep_slots(h, left(k), slots[0, h, k])
    for t in range(tiles):
        if t == tiles - 1:
            take_sibling(0, t, handed[t])
        value = multiply_tile(rows_of(t), slice(None))
        for e in range(cap):
            for h in range(halves):
                x_buf[h, t * cap + e] = value[e * b:(e + 1) * b, h * LANES:(h + 1) * LANES]
    x_copies = {}
    for h in range(halves):
        for k in range(1, n_rows):
            pack(1, h, k, x_rows)
            x_copies[h, k] = send_slots(1, h, k)
    for h in range(halves):
        pack(1, h, 0, x_rows)
        keep_slots(h, me, packed[1, h, 0])

    handed = []
    for t in range(tiles):
        handed.append(arrive(1, t, p_cross[t]))
        keep(mine, t, total[1, :, rows_of(t)])
    for t in range(tiles):
        take_sibling(1, t, handed[t])

    for h in range(halves):
        lanes = slice(h * LANES, (h + 1) * LANES)
        for k in range(1, n_rows):
            x_copies[h, k].wait_recv()
            keep_slots(h, left(k), slots[1, h, k])
        for t in range(tiles):
            out[rows_of(t), lanes] = multiply_tile(rows_of(t), lanes)
    for copy in started:
        copy.wait_send()


def merged_body(n_rows, n_cols, h_blocks, p_blocks, h_fetch, p_fetch, h_slot, p_slot, p_panel):
    cap, b = h_fetch.shape[2], h_blocks.shape[2]
    rows_all, columns = p_panel.shape
    depth, per_half, halves = cap * b, n_rows // 2, columns // LANES
    tiles = rows_all // depth
    f32, bf16, dma = jnp.float32, jnp.bfloat16, pltpu.SemaphoreType.DMA
    exchanged = pltpu.VMEM((2, per_half, rows_all, depth), f32)
    slots_and_lists = (h_slot, p_slot, jnp.swapaxes(h_fetch, 1, 2), jnp.swapaxes(p_fetch, 1, 2))
    vmem, smem = pl.BlockSpec(memory_space=pltpu.VMEM), pl.BlockSpec(memory_space=pltpu.SMEM)
    return pl.pallas_call(
        functools.partial(product_kernel, n_rows, n_cols, cap, b),
        out_shape=pltpu.VMEM((rows_all, columns), f32),
        in_specs=[smem] * 4 + [pl.BlockSpec(memory_space=pltpu.HBM)] * 2 + [vmem],
        out_specs=vmem,
        scratch_shapes=[
            pltpu.VMEM((2, *h_blocks.shape), f32),
            pltpu.VMEM((2, n_rows, rows_all, depth), f32),
            pltpu.VMEM((n_rows, 1, LANES), jnp.int32),
            pltpu.VMEM((n_rows, 1, LANES), jnp.int32),
            pltpu.SMEM((n_rows, 1, LANES), jnp.int32),
            exchanged, exchanged, exchanged, exchanged, exchanged,
            pltpu.VMEM((rows_all, n_rows * depth), bf16),
            pltpu.VMEM((rows_all, n_rows * depth), bf16),
            pltpu.VMEM((2, halves, n_rows, depth, LANES), f32),
            pltpu.VMEM((2, halves, n_rows, depth, LANES), f32),
            pltpu.VMEM((n_rows * depth, columns), bf16),
            pltpu.VMEM((n_rows * depth, columns), bf16),
            pltpu.VMEM((halves, rows_all // b, b, LANES), f32),
            dma((2, tiles)), dma((n_rows,)), dma((n_rows,)), dma,
            dma((2, tiles)), dma((2, tiles)),
            dma((2, tiles)), dma((2, tiles)),
            dma((2, tiles)), dma((2, tiles)),
            dma((2, halves, n_rows)), dma((2, halves, n_rows)),
        ],
        compiler_params=pltpu.CompilerParams(
            collective_id=0, has_side_effects=True, vmem_limit_bytes=58 * 1024 * 1024
        ),
        name="product",
    )(*slots_and_lists, h_blocks, p_blocks, p_panel.reshape(-1, b, columns))


def solution(mesh):
    n_rows, n_cols = mesh.shape["rows"], mesh.shape["cols"]
    in_specs = (
        P("rows", "cols", None, None),
        P("rows", "cols", None, None),
        P("rows", None, None),
        P("rows", None, None),
        P("rows", None),
        P("rows", None),
        P("rows", "cols"),
    )
    out_specs = P("rows", "cols")

    def body(h_blocks, p_blocks, h_fetch, p_fetch, h_slot, p_slot, p_panel):
        cap, b = h_fetch.shape[2], h_blocks.shape[2]
        fits = n_cols == 4 and n_rows % 2 == 0 and cap * b == LANES and h_blocks.shape[0] % cap == 0 and p_panel.shape[1] % LANES == 0
        arguments = (h_blocks, p_blocks, h_fetch, p_fetch, h_slot, p_slot, p_panel)
        if fits and cap * n_rows <= h_slot.shape[1]:
            return merged_body(n_rows, n_cols, *arguments)
        return list_body(*arguments)

    return jax.shard_map(body, mesh=mesh, in_specs=in_specs, out_specs=out_specs, check_vma=False)
```
